512 devices in a mesh: span: 8 (over z_lo, core), seq: 64 (over y, x, z_hi).
Axes of the slice: x: 4, y: 4, z: 16 (z_hi: 4, z_lo: 4; z = z_hi * 4 + z_lo), core: 2. Of those that a mesh axis runs over, the one named last changes fastest.
Arguments:
- query_rows: bfloat16 [8, 512, 4096], P('span', 'seq'), may hold values from -6 to 6
- key_rows: bfloat16 [8, 512, 4096], P('span', 'seq'), may hold values from -6 to 6
- value_rows: bfloat16 [8, 512, 4096], P('span', 'seq'), may hold values from -6 to 6
- counts: int32 [8], replicated, may hold values from 128 to 512, as said below
- levels: int32 [8], replicated, may hold values from 0 to 63
- gate_table: float32 [64, 4096], replicated, may hold values from 0.1 to 1.9
Outputs:
- mixed_rows: bfloat16 [8, 512, 4096], P('span', 'seq')
The draws below stay inside these ranges and needn't reach their ends.
Inputs may be any that keep to these rules, and one draw needn't show every extreme that they name: `counts`: some span has all 512 tokens live in every draw.
All inputs are finite; a program needn't handle non-finite values.
Results may differ from the reference program's by a relative error of at most 0.0075.
Values may be sent and summed in bfloat16 or wider, within the bound.
A program may use at most 64 MiB of HBM per device.

```python
import math
import jax
import jax.numpy as jnp
from jax import lax

HEADS = 32
HEAD_DIM = 128
LEVELS = 64
SPANS = 8
SPAN_TOK = 512
WIDTH = 4096


def draw_query_rows(key, part):
    key = jax.random.fold_in(key, 1)
    full_shape = (SPANS, SPAN_TOK, HEADS * HEAD_DIM)
    values = jnp.clip(jax.random.normal(jax.random.fold_in(key, 2), full_shape, jnp.float32), -6.0, 6.0)
    return values.astype(jnp.bfloat16)


def draw_key_rows(key, part):
    key = jax.random.fold_in(key, 5)
    full_shape = (SPANS, SPAN_TOK, HEADS * HEAD_DIM)
    values = jnp.clip(jax.random.normal(jax.random.fold_in(key, 2), full_shape, jnp.float32), -6.0, 6.0)
    return values.astype(jnp.bfloat16)


def draw_counts(key, part):
    key = jax.random.fold_in(key, 9)
    drawn = jax.random.randint(jax.random.fold_in(key, 1), (SPANS,), SPAN_TOK // 4, SPAN_TOK + 1)
    full_one = jax.random.randint(jax.random.fold_in(key, 2), (), 0, SPANS)
    return jnp.where(jnp.arange(SPANS, dtype=jnp.int32) == full_one, SPAN_TOK, drawn).astype(jnp.int32)


def set_ends(result, own_key, least, largest):
    longest = result.shape.index(max(result.shape))
    spots = []
    for shift in (0, 1):
        where = [jax.random.randint(jax.random.fold_in(own_key, axis), (), 0, length) for axis, length in enumerate(result.shape)]
        where[longest] = (where[longest] + shift) % result.shape[longest]
        spots.append(tuple(where))
    return result.at[spots[0]].set(least).at[spots[1]].set(largest)


def block_scale(own_key, shape, cuts, least, top_value):
    gain = 1.0
    for axis_at, blocks in cuts:
        draws = jax.random.uniform(jax.random.fold_in(jax.random.fold_in(own_key, 6), axis_at), (blocks,), jnp.float32, least / len(cuts), top_value / len(cuts))
        gain = gain * jnp.repeat(jnp.exp(draws), shape[axis_at] // blocks).reshape((-1,) + (1,) * (len(shape) - 1 - axis_at))
    return gain


def scatter_about(own_key, shape, spread, reach, pieces=(), kind=jnp.bfloat16):
    values = jax.random.normal(own_key, shape, jnp.float32) * spread
    if len(pieces) > 0:
        values = block_scale(own_key, shape, pieces, -0.22, 0.18) * values
    return jnp.clip(values, min=-reach, max=reach).astype(kind)


def setup_inputs(seed: int = 0) -> dict:
    key_list = jax.random.split(jax.random.key(seed), 7)
    return {
        "query_rows": draw_query_rows(jax.random.fold_in(key_list[6], 71), 0),
        "key_rows": draw_key_rows(jax.random.fold_in(key_list[6], 71), 0),
        "value_rows": scatter_about(key_list[2], (SPANS, SPAN_TOK, WIDTH), 1.0, 6.0, ((0, 8), (1, 64))),
        "counts": draw_counts(jax.random.fold_in(key_list[6], 71), 0),
        "levels": set_ends(jax.random.randint(key_list[4], (SPANS,), 0, LEVELS), jax.random.fold_in(key_list[4], 1), 0, LEVELS - 1).astype(jnp.int32),
        "gate_table": jnp.clip(1.0 + 0.18 * jax.random.normal(key_list[5], (LEVELS, WIDTH), jnp.float32), 0.1, 1.9),
    }


epsilon = 1e-05
masked_score = -1e+30

def head_attend(query_head, key_head, value_head, allowed, gate_head):
    score_scale = 1.0 / math.sqrt(HEAD_DIM)
    scores = jnp.dot(query_head.astype(jnp.float32), key_head.astype(jnp.float32).T, preferred_element_type=jnp.float32) * score_scale
    scores = jnp.where(allowed[None, :], scores, masked_score)
    top_score = lax.optimization_barrier(jnp.max(scores, axis=1, keepdims=True))
    weights = jnp.where(allowed[None, :], jnp.exp(scores - top_score), 0.0)
    weight_total = lax.optimization_barrier(jnp.sum(weights, axis=1, keepdims=True))
    rounded = weights.astype(jnp.bfloat16)
    attended = jnp.dot(rounded.astype(jnp.float32), value_head.astype(jnp.float32), preferred_element_type=jnp.float32) / weight_total
    normed = attended * lax.rsqrt(lax.optimization_barrier(jnp.mean(attended * attended, axis=1, keepdims=True)) + epsilon)
    return (normed * gate_head[None, :]).astype(jnp.bfloat16)

def reference(query_rows, key_rows, value_rows, counts, levels, gate_table):
    key_heads = key_rows.reshape(SPANS * SPAN_TOK, HEADS, HEAD_DIM).transpose(1, 0, 2)
    value_heads = value_rows.reshape(SPANS * SPAN_TOK, HEADS, HEAD_DIM).transpose(1, 0, 2)
    positions = jnp.arange(SPAN_TOK, dtype=jnp.int32)
    live_keys = positions[None, :] < counts[:, None]
    span_ids = jnp.arange(SPANS, dtype=jnp.int32)

    def one_span(span_index):
        query_span = lax.dynamic_index_in_dim(query_rows, span_index, 0, keepdims=False)
        query_heads = query_span.reshape(SPAN_TOK, HEADS, HEAD_DIM).transpose(1, 0, 2)
        allowed = ((span_ids[:, None] <= span_index) & live_keys).reshape(SPANS * SPAN_TOK)
        noise_level = lax.dynamic_index_in_dim(levels, span_index, 0, keepdims=False)
        gate_row = lax.dynamic_index_in_dim(gate_table, noise_level, 0, keepdims=False).reshape(HEADS, HEAD_DIM)

        def one_head(inputs):
            return head_attend(inputs[0], inputs[1], inputs[2], allowed, inputs[3])
        mixed_heads = lax.map(one_head, (query_heads, key_heads, value_heads, gate_row))
        return mixed_heads.transpose(1, 0, 2).reshape(SPAN_TOK, HEADS * HEAD_DIM)
    return lax.map(one_span, jnp.arange(SPANS, dtype=jnp.int32))
```

```python
import functools
import math

import jax
import jax.numpy as jnp
from jax import lax
from jax.experimental import pallas as pl
from jax.experimental.pallas import tpu as pltpu
from jax.sharding import PartitionSpec as P

HEAD_DIM = 128
EPSILON = 1e-5
MASKED = -1e30
LOWEST = -1e4
TINY = 1e-30
MESH = pl.DeviceIdType.MESH


def kernel(
    spans, z_far, side, tok,
    query_ref, key_ref, value_ref, counts_ref, levels_ref, gate_ref, out_ref,
    key_in, query_in, value_in, key_all, query_all, value_all, part, part_in, lse, lse_in,
    mixed, gate_v,
    send_sem, recv_sem, own_sem, key_sems, query_sems, value_sems, part_sems, lse_sems,
    out_send, out_recv, out_own, gate_sem,
):
    column = spans * z_far
    rows = z_far * tok
    span = lax.axis_index("span")
    seq = lax.axis_index("seq")
    z_hi = lax.rem(seq, z_far)
    plane = lax.div(seq, z_far)
    row_y, col_x = lax.div(plane, side), lax.rem(plane, side)
    core = lax.rem(span, 2)
    place = z_hi * spans + span
    key_at = jnp.where(core == 0, row_y, col_x)
    query_at = jnp.where(core == 0, col_x, row_y)
    key_step = jnp.where(core == 0, side, 1)
    query_step = jnp.where(core == 0, 1, side)
    slot = span * z_far + z_hi

    def at_place(other):
        other_hi, other_span = lax.div(other, spans), lax.rem(other, spans)
        return {"span": other_span, "seq": plane * z_far + other_hi}

    def other_place(step):
        half = lax.div(step + 1, 2)
        away = column // 2 + jnp.where(lax.rem(step, 2) == 0, half, -half)
        return lax.rem(place + away, column)

    def key_peer(turn):
        other = lax.rem(key_at + turn, side)
        return other, {"span": span, "seq": seq + (other - key_at) * key_step * z_far}

    def query_peer(turn):
        other = lax.rem(query_at + turn, side)
        return other, {"span": span, "seq": seq + (other - query_at) * query_step * z_far}

    def channels(head):
        return pl.ds(pl.multiple_of(head * HEAD_DIM, HEAD_DIM), HEAD_DIM)

    pairs = ((key_ref, key_in, 0), (query_ref, query_in, 1), (value_ref, value_in, 2))

    barrier = pltpu.get_barrier_semaphore()

    def greet(step, carry):
        pl.semaphore_signal(barrier, inc=1, device_id=at_place(other_place(step)), device_id_type=MESH)
        return carry

    lax.fori_loop(0, column - 1, greet, 0)
    for turn in range(1, side):
        pl.semaphore_signal(barrier, inc=1, device_id=key_peer(turn)[1], device_id_type=MESH)
        pl.semaphore_signal(barrier, inc=1, device_id=query_peer(turn)[1], device_id_type=MESH)

    gate_copy = pltpu.make_async_copy(gate_ref.at[:, channels(place)], gate_v, gate_sem)
    gate_copy.start()
    own = []
    for source, target, n in pairs:
        copy = pltpu.make_async_copy(source.at[0, :, channels(place)], target.at[slot], own_sem.at[n])
        copy.start()
        own.append(copy)
    pl.semaphore_wait(barrier, column - 1 + 2 * (side - 1))

    for source, target, n in pairs:
        def spread(step, carry, source=source, target=target, n=n):
            other = other_place(step)
            pltpu.make_async_remote_copy(
                src_ref=source.at[0, :, channels(other)], dst_ref=target.at[slot],
                send_sem=send_sem.at[n], recv_sem=recv_sem.at[n],
                device_id=at_place(other), device_id_type=MESH,
            ).start()
            return carry
        lax.fori_loop(0, column - 1, spread, 0)

    def arrived(target, n):
        own[n].wait()
        rest = target.at[pl.ds(0, column - 1)]
        pltpu.make_async_copy(rest, rest, recv_sem.at[n]).wait()
        whole = target[...].astype(jnp.float32).reshape(spans, rows, HEAD_DIM)
        return whole.astype(jnp.bfloat16)

    def gather(block, target, sems, peer, here):
        target[:, here] = block
        copies = []
        for turn in range(1, side):
            copy = pltpu.make_async_remote_copy(
                src_ref=target.at[:, here], dst_ref=target.at[:, here],
                send_sem=sems.at[0, turn], recv_sem=sems.at[1, turn],
                device_id=peer(turn)[1], device_id_type=MESH,
            )
            copy.start()
            copies.append(copy)
        return copies

    key_copies = gather(arrived(key_in, 0), key_all, key_sems, key_peer, key_at)
    query_copies = gather(arrived(query_in, 1), query_all, query_sems, query_peer, query_at)
    value_copies = gather(arrived(value_in, 2), value_all, value_sems, key_peer, key_at)
    for copy in key_copies + query_copies + value_copies:
        copy.wait()

    many = side * rows
    lanes = lax.broadcasted_iota(jnp.int32, (1, many), 1)
    position = (plane + (lax.div(lanes, rows) - key_at) * key_step) * rows + lax.rem(lanes, rows)
    bias = jnp.concatenate(
        [jnp.where(position < counts_ref[c], 0.0, MASKED) for c in range(spans)], axis=1
    )
    diagonal = lax.broadcasted_iota(jnp.int32, (many, many), 0) == lax.broadcasted_iota(
        jnp.int32, (many, many), 1
    )
    factor = math.log2(math.e) / math.sqrt(HEAD_DIM)
    for i in range(spans):
        wide = (i + 1) * many
        queries = query_all[i].reshape(many, HEAD_DIM)
        keys = key_all[0 : i + 1].reshape(wide, HEAD_DIM)
        values = value_all[0 : i + 1].reshape(wide, HEAD_DIM)
        scores = lax.dot_general(
            queries, keys, (((1,), (1,)), ((), ())), preferred_element_type=jnp.float32
        )
        scores = scores * factor + bias[:, :wide]
        top = jnp.maximum(jnp.max(scores, axis=1, keepdims=True), LOWEST)
        weights = jnp.exp2(scores - top)
        total = jnp.maximum(jnp.sum(weights, axis=1, keepdims=True), TINY)
        mix = jnp.dot(weights.astype(jnp.bfloat16), values, preferred_element_type=jnp.float32)
        part[:, i] = (mix / total).astype(jnp.bfloat16).reshape(side, rows, HEAD_DIM)
        column_lse = top + jnp.log2(total)
        lse[i : i + 1, :] = jnp.sum(jnp.where(diagonal, column_lse, 0.0), axis=0, keepdims=True)

    copies = []
    for turn in range(1, side):
        other, peer = query_peer(turn)
        for source, target, sems in (
            (part.at[other], part_in.at[turn - 1], part_sems),
            (lse, lse_in.at[turn - 1], lse_sems),
        ):
            copy = pltpu.make_async_remote_copy(
                src_ref=source, dst_ref=target, send_sem=sems.at[0, turn], recv_sem=sems.at[1, turn],
                device_id=peer, device_id_type=MESH,
            )
            copy.start()
            copies.append(copy)
    gate_copy.wait()
    for copy in copies:
        copy.wait()

    tables = [lse[...]] + [lse_in[n] for n in range(side - 1)]
    top = functools.reduce(jnp.maximum, tables)
    tables = [jnp.exp2(table - top) for table in tables]
    total = functools.reduce(jnp.add, tables)
    tables = [table / total for table in tables]
    mine = lax.broadcasted_iota(jnp.int32, (rows, many), 1) == (
        query_at * rows + lax.broadcasted_iota(jnp.int32, (rows, many), 0)
    )
    for i in range(spans):
        attended = jnp.zeros((rows, HEAD_DIM), jnp.float32)
        for n in range(side):
            block = part[query_at, i] if n == 0 else part_in[n - 1, i]
            share = jnp.sum(jnp.where(mine, tables[n][i : i + 1], 0.0), axis=1, keepdims=True)
            attended = attended + share * block.astype(jnp.float32)
        mean = jnp.mean(attended * attended, axis=1, keepdims=True)
        gate = gate_v[pl.ds(levels_ref[i], 1), :]
        normed = attended * lax.rsqrt(mean + EPSILON) * gate
        mixed[i * z_far : (i + 1) * z_far] = normed.reshape(z_far, tok, HEAD_DIM).astype(jnp.bfloat16)

    back = pltpu.make_async_copy(mixed.at[slot], out_ref.at[0, :, channels(place)], out_own)
    back.start()

    def send_back(step, carry):
        other = other_place(step)
        other_slot = lax.rem(other, spans) * z_far + lax.div(other, spans)
        pltpu.make_async_remote_copy(
            src_ref=mixed.at[other_slot], dst_ref=out_ref.at[0, :, channels(place)],
            send_sem=out_send, recv_sem=out_recv, device_id=at_place(other), device_id_type=MESH,
        ).start()
        return carry

    lax.fori_loop(0, column - 1, send_back, 0)
    for n in range(3):
        rest = key_in.at[pl.ds(0, column - 1)]
        pltpu.make_async_copy(rest, rest, send_sem.at[n]).wait()
    rest = mixed.at[pl.ds(0, column - 1)]
    pltpu.make_async_copy(rest, rest, out_send).wait()
    back.wait()
    rest = out_ref.at[0, :, pl.ds(0, (column - 1) * HEAD_DIM)]
    pltpu.make_async_copy(rest, rest, out_recv).wait()


def body(query_rows, key_rows, value_rows, counts, levels, gate_table):
    spans = lax.axis_size("span")
    seq_size = lax.axis_size("seq")
    tok, width = query_rows.shape[1:]
    column = width // HEAD_DIM
    z_far = column // spans
    side = math.isqrt(seq_size // z_far)
    rows = z_far * tok
    bf16, f32 = jnp.bfloat16, jnp.float32
    landing = pltpu.VMEM((column, tok, HEAD_DIM), bf16)
    gathered = pltpu.VMEM((spans, side, rows, HEAD_DIM), bf16)
    dma = pltpu.SemaphoreType.DMA
    anywhere = pl.BlockSpec(memory_space=pl.ANY)
    scalars = pl.BlockSpec(memory_space=pltpu.SMEM)
    return pl.pallas_call(
        functools.partial(kernel, spans, z_far, side, tok),
        out_shape=jax.ShapeDtypeStruct(query_rows.shape, bf16),
        in_specs=[anywhere, anywhere, anywhere, scalars, scalars, anywhere],
        out_specs=anywhere,
        scratch_shapes=[
            landing, landing, landing, gathered, gathered, gathered,
            pltpu.VMEM((side, spans, rows, HEAD_DIM), bf16),
            pltpu.VMEM((side - 1, spans, rows, HEAD_DIM), bf16),
            pltpu.VMEM((spans, side * rows), f32),
            pltpu.VMEM((side - 1, spans, side * rows), f32),
            landing,
            pltpu.VMEM((gate_table.shape[0], HEAD_DIM), f32),
            dma((3,)), dma((3,)), dma((3,)),
            dma((2, side)), dma((2, side)), dma((2, side)), dma((2, side)), dma((2, side)),
            dma, dma, dma, dma,
        ],
        compiler_params=pltpu.CompilerParams(
            collective_id=0, has_side_effects=True, vmem_limit_bytes=32 * 1024 * 1024
        ),
        cost_estimate=pl.CostEstimate(
            flops=600_000_000, bytes_accessed=1_000_000, transcendentals=600_000
        ),
    )(query_rows, key_rows, value_rows, counts, levels, gate_table)


def solution(mesh):
    placed = (P("span", "seq", None), P("span", "seq", None), P("span", "seq", None), P(), P(), P())
    return jax.shard_map(
        body, mesh=mesh, in_specs=placed, out_specs=P("span", "seq", None), check_vma=False
    )
```

```python
import functools
import math

import jax
import jax.numpy as jnp
from jax import lax
from jax.experimental import pallas as pl
from jax.experimental.pallas import tpu as pltpu
from jax.sharding import PartitionSpec as P

HEAD_DIM = 128
EPSILON = 1e-5
MASKED = -1e30
LOWEST = -1e4
TINY = 1e-30
MESH = pl.DeviceIdType.MESH
VMEM_BYTES = 32 * 1024 * 1024


def kernel(
    spans, z_far, side, tok,
    query_ref, key_ref, value_ref, counts_ref, levels_ref, gate_ref, out_ref,
    key_all, query_all, value_all, keys_flat, values_flat, chances, part, part_in, lse, lse_in,
    mixed, gate_v, counts_s, levels_s,
    send_sem, recv_sem, key_sems, query_sems, value_sems, part_sems, lse_sems,
    out_send, out_recv, small_sems,
):
    column = spans * z_far
    half_size = column // 2
    near = z_far // 2
    rows = z_far * tok
    many = side * rows
    pairs = spans // 2
    span = lax.axis_index("span")
    seq = lax.axis_index("seq")
    z_hi = lax.rem(seq, z_far)
    plane = lax.div(seq, z_far)
    row_y, col_x = lax.div(plane, side), lax.rem(plane, side)
    core = lax.rem(span, 2)
    place = z_hi * spans + span
    key_at = jnp.where(core == 0, row_y, col_x)
    query_at = jnp.where(core == 0, col_x, row_y)
    key_step = jnp.where(core == 0, side, 1)
    query_step = jnp.where(core == 0, 1, side)
    my_half = lax.div(place, half_size)

    def at_place(other):
        return {"span": lax.rem(other, spans), "seq": plane * z_far + lax.div(other, spans)}

    def other_place(step):
        half = lax.div(step + 1, 2)
        away = column // 2 + jnp.where(lax.rem(step, 2) == 0, half, -half)
        return lax.rem(place + away, column)

    def key_peer(turn):
        other = lax.rem(key_at + turn, side)
        return {"span": span, "seq": seq + (other - key_at) * key_step * z_far}

    def query_peer(turn):
        other = lax.rem(query_at + turn, side)
        return {"span": span, "seq": seq + (other - query_at) * query_step * z_far}

    def channels(head):
        return pl.ds(pl.multiple_of(head * HEAD_DIM, HEAD_DIM), HEAD_DIM)

    barrier = pltpu.get_barrier_semaphore()

    def greet(step, carry):
        pl.semaphore_signal(barrier, inc=1, device_id=at_place(other_place(step)), device_id_type=MESH)
        return carry

    lax.fori_loop(0, column - 1, greet, 0)
    for turn in range(1, side):
        pl.semaphore_signal(barrier, inc=1, device_id=key_peer(turn), device_id_type=MESH)
        pl.semaphore_signal(barrier, inc=1, device_id=query_peer(turn), device_id_type=MESH)

    arrays = ((key_ref, key_all, 0), (query_ref, query_all, 1), (value_ref, value_all, 2))
    for source, target, n in arrays:
        here = query_at if n == 1 else key_at
        pltpu.make_async_copy(
            source.at[0, :, channels(place)], target.at[here, z_hi, span], recv_sem.at[n, my_half]
        ).start()
    small = [
        pltpu.make_async_copy(counts_ref, counts_s, small_sems.at[0]),
        pltpu.make_async_copy(levels_ref, levels_s, small_sems.at[1]),
        pltpu.make_async_copy(gate_ref.at[:, channels(place)], gate_v, small_sems.at[2]),
    ]
    for copy in small:
        copy.start()
    pl.semaphore_wait(barrier, column - 1 + 2 * (side - 1))

    for source, target, n in arrays:
        def spread(step, carry, source=source, target=target, n=n):
            other = other_place(step)
            along = lax.rem(other, 2) == 0
            there = jnp.where(along, col_x, row_y) if n == 1 else jnp.where(along, row_y, col_x)
            pltpu.make_async_remote_copy(
                src_ref=source.at[0, :, channels(other)], dst_ref=target.at[there, z_hi, span],
                send_sem=send_sem.at[n], recv_sem=recv_sem.at[n, my_half],
                device_id=at_place(other), device_id_type=MESH,
            ).start()
            return carry
        lax.fori_loop(0, column - 1, spread, 0)

    def gather(n, half):
        target = arrays[n][1]
        here, peer = (query_at, query_peer) if n == 1 else (key_at, key_peer)
        sems = (key_sems, query_sems, value_sems)[n]
        block = target.at[here, pl.ds(half * near, near)]
        pltpu.make_async_copy(block, block, recv_sem.at[n, half]).wait()
        copies = []
        for turn in range(1, side):
            copy = pltpu.make_async_remote_copy(
                src_ref=block, dst_ref=block, send_sem=sems.at[0, half, turn],
                recv_sem=sems.at[1, half, turn], device_id=peer(turn), device_id_type=MESH,
            )
            copy.start()
            copies.append(copy)
        return copies

    sent = []
    scoring = gather(0, 1) + gather(1, 1) + gather(0, 0) + gather(1, 0)
    mixing = gather(2, 1) + gather(2, 0)
    sent += scoring + mixing

    lanes = lax.broadcasted_iota(jnp.int32, (1, many), 1)
    position = (plane + (lax.div(lanes, rows) - key_at) * key_step) * rows + lax.rem(lanes, rows)
    for copy in small:
        copy.wait()
    bias = jnp.concatenate(
        [jnp.where(position < counts_s[c], 0.0, MASKED) for c in range(spans)], axis=1
    )
    row_ids = lax.broadcasted_iota(jnp.int32, (many, many), 0)
    diagonal = row_ids == lax.broadcasted_iota(jnp.int32, (many, many), 1)
    later = jnp.where(lax.rem(lax.div(row_ids, tok), 2) == 0, MASKED, 0.0)
    factor = math.log2(math.e) / math.sqrt(HEAD_DIM)

    for copy in scoring:
        copy.wait_recv()

    def flat(tiles):
        wide = tiles.astype(jnp.float32)
        return wide.reshape(math.prod(wide.shape[:-1]), HEAD_DIM).astype(jnp.bfloat16)

    def flatten(source, target):
        for c in range(spans):
            target[c * many : (c + 1) * many] = flat(source[:, :, c])

    def score(half):
        totals = []
        for j in range(pairs):
            wide = 2 * (j + 1) * many
            queries = flat(query_all[:, half * near : (half + 1) * near, 2 * j : 2 * j + 2])
            scores = lax.dot_general(
                queries, keys_flat[:wide], (((1,), (1,)), ((), ())),
                preferred_element_type=jnp.float32,
            )
            scores = scores * factor + bias[:, :wide]
            scores = jnp.concatenate([scores[:, : wide - many], scores[:, wide - many :] + later], axis=1)
            top = jnp.maximum(jnp.max(scores, axis=1, keepdims=True), LOWEST)
            weights = jnp.exp2(scores - top)
            total = jnp.maximum(jnp.sum(weights, axis=1, keepdims=True), TINY)
            chances[half, j, :, :wide] = weights.astype(jnp.bfloat16)
            both = jnp.sum(jnp.where(diagonal, top + jnp.log2(total), 0.0), axis=0, keepdims=True)
            lse[half, j : j + 1, :] = both
            lse[half, pairs + j : pairs + j + 1, :] = both
            totals.append(1.0 / total)
        return totals

    def mix(half, totals):
        for j in range(pairs):
            wide = 2 * (j + 1) * many
            mixture = jnp.dot(
                chances[half, j, :, :wide], values_flat[:wide], preferred_element_type=jnp.float32
            )
            mixture = (mixture * totals[j]).reshape(side, near, 2, tok, HEAD_DIM)
            part[half, :, :, 2 * j : 2 * j + 2] = mixture.astype(jnp.bfloat16)
        copies = []
        for turn in range(1, side):
            other = lax.rem(query_at + turn, side)
            for source, target, sems in (
                (part.at[half, other], part_in.at[half, turn - 1], part_sems),
                (lse.at[half], lse_in.at[half, turn - 1], lse_sems),
            ):
                copy = pltpu.make_async_remote_copy(
                    src_ref=source, dst_ref=target, send_sem=sems.at[0, half, turn],
                    recv_sem=sems.at[1, half, turn], device_id=query_peer(turn), device_id_type=MESH,
                )
                copy.start()
                copies.append(copy)
        return copies

    flatten(key_all, keys_flat)
    totals = [score(0), score(1)]
    for copy in mixing:
        copy.wait_recv()
    flatten(value_all, values_flat)
    parts = [mix(0, totals[0]), mix(1, totals[1])]
    sent += parts[0] + parts[1]

    cut = 2 * near * tok
    mine = lax.broadcasted_iota(jnp.int32, (cut, many), 1) == (
        query_at * cut + lax.broadcasted_iota(jnp.int32, (cut, many), 0)
    )
    second = lax.rem(lax.div(lax.broadcasted_iota(jnp.int32, (cut, 1), 0), tok), 2) == 1

    def finish(half):
        for copy in parts[half]:
            copy.wait_recv()
        tables = [lse[half]] + [lse_in[half, n] for n in range(side - 1)]
        top = functools.reduce(jnp.maximum, tables)
        tables = [jnp.exp2(table - top) for table in tables]
        total = functools.reduce(jnp.add, tables)
        tables = [table / total for table in tables]
        for j in range(pairs):
            pick = slice(2 * j, 2 * j + 2)
            attended = jnp.zeros((cut, HEAD_DIM), jnp.float32)
            for n in range(side):
                tile = part[half, query_at, :, pick] if n == 0 else part_in[half, n - 1, :, pick]
                share = jnp.sum(jnp.where(mine, tables[n][j : j + 1], 0.0), axis=1, keepdims=True)
                attended = attended + share * tile.astype(jnp.float32).reshape(cut, HEAD_DIM)
            mean = jnp.mean(attended * attended, axis=1, keepdims=True)
            gate = jnp.where(
                second,
                gate_v[pl.ds(levels_s[2 * j + 1], 1), :],
                gate_v[pl.ds(levels_s[2 * j], 1), :],
            )
            normed = attended * lax.rsqrt(mean + EPSILON) * gate
            mixed[half * near : (half + 1) * near, pick] = normed.reshape(
                near, 2, tok, HEAD_DIM
            ).astype(jnp.bfloat16)

        def send_back(step, carry):
            away = half_size // 2 + jnp.where(
                lax.rem(step, 2) == 0, lax.div(step + 1, 2), -lax.div(step + 1, 2)
            )
            other = half * half_size + lax.rem(place + away + half_size, half_size)

            @pl.when(other != place)
            def _():
                pltpu.make_async_remote_copy(
                    src_ref=mixed.at[lax.div(other, spans), lax.rem(other, spans)],
                    dst_ref=out_ref.at[0, :, channels(place)],
                    send_sem=out_send, recv_sem=out_recv,
                    device_id=at_place(other), device_id_type=MESH,
                ).start()

            @pl.when(other == place)
            def _():
                pltpu.make_async_copy(
                    mixed.at[z_hi, span], out_ref.at[0, :, channels(place)], out_recv
                ).start()

            return carry

        lax.fori_loop(0, half_size, send_back, 0)

    finish(0)
    finish(1)
    for source, target, n in arrays:
        rest = source.at[0, :, pl.ds(0, (column - 1) * HEAD_DIM)]
        pltpu.make_async_copy(rest, rest, send_sem.at[n]).wait()
    for copy in sent:
        copy.wait_send()
    rest = out_ref.at[0, :, pl.ds(0, (column - 1) * HEAD_DIM)]
    pltpu.make_async_copy(rest, rest, out_send).wait()
    pltpu.make_async_copy(out_ref, out_ref, out_recv).wait()


def body(query_rows, key_rows, value_rows, counts, levels, gate_table):
    spans = lax.axis_size("span")
    seq_size = lax.axis_size("seq")
    tok, width = query_rows.shape[1:]
    column = width // HEAD_DIM
    z_far = column // spans
    side = math.isqrt(seq_size // z_far)
    many = side * z_far * tok
    pairs = spans // 2
    bf16, f32 = jnp.bfloat16, jnp.float32
    gathered = pltpu.VMEM((side, z_far, spans, tok, HEAD_DIM), bf16)
    flat = pltpu.VMEM((spans * many, HEAD_DIM), bf16)
    dma = pltpu.SemaphoreType.DMA
    hbm = pl.BlockSpec(memory_space=pltpu.HBM)
    return pl.pallas_call(
        functools.partial(kernel, spans, z_far, side, tok),
        out_shape=jax.ShapeDtypeStruct(query_rows.shape, bf16),
        in_specs=[hbm] * 6,
        out_specs=pl.BlockSpec(memory_space=pl.ANY),
        scratch_shapes=[
            gathered, gathered, gathered, flat, flat,
            pltpu.VMEM((2, pairs, many, spans * many), bf16),
            pltpu.VMEM((2, side, z_far // 2, spans, tok, HEAD_DIM), bf16),
            pltpu.VMEM((2, side - 1, z_far // 2, spans, tok, HEAD_DIM), bf16),
            pltpu.VMEM((2, 2 * pairs, many), f32),
            pltpu.VMEM((2, side - 1, 2 * pairs, many), f32),
            pltpu.VMEM((z_far, spans, tok, HEAD_DIM), bf16),
            pltpu.VMEM((gate_table.shape[0], HEAD_DIM), f32),
            pltpu.SMEM(counts.shape, jnp.int32),
            pltpu.SMEM(levels.shape, jnp.int32),
            dma((3,)), dma((3, 2)),
            dma((2, 2, side)), dma((2, 2, side)), dma((2, 2, side)),
            dma((2, 2, side)), dma((2, 2, side)),
            dma, dma, dma((3,)),
        ],
        compiler_params=pltpu.CompilerParams(
            collective_id=0, has_side_effects=True, vmem_limit_bytes=VMEM_BYTES
        ),
        cost_estimate=pl.CostEstimate(
            flops=600_000_000, bytes_accessed=1_000_000, transcendentals=700_000
        ),
    )(*[
        pltpu.with_memory_space_constraint(array, pltpu.HBM)
        for array in (query_rows, key_rows, value_rows, counts, levels, gate_table)
    ])


def solution(mesh):
    placed = (P("span", "seq", None), P("span", "seq", None), P("span", "seq", None), P(), P(), P())
    return jax.shard_map(
        body, mesh=mesh, in_specs=placed, out_specs=P("span", "seq", None), check_vma=False
    )
```

```python
import functools
import math

import jax
import jax.numpy as jnp
from jax import lax
from jax.experimental import pallas as pl
from jax.experimental.pallas import tpu as pltpu
from jax.sharding import PartitionSpec as P

HEAD_DIM = 128
EPSILON = 1e-5
MASKED = -1e30
LOWEST = -1e4
TINY = 1e-30
MESH = pl.DeviceIdType.MESH
VMEM_BYTES = 32 * 1024 * 1024


def kernel(
    spans, z_far, side, tok,
    query_ref, key_ref, value_ref, counts_ref, levels_ref, gate_ref, out_ref,
    key_all, query_all, value_all, keys_flat, values_flat, chances, summed, part, part_in, lse, lse_in,
    mixed, gate_v, counts_s, levels_s,
    send_sem, recv_sem, key_sems, query_sems, value_sems, part_sems, lse_sems,
    out_send, out_recv, small_sems,
):
    column = spans * z_far
    half_size = column // 2
    near = z_far // 2
    rows = z_far * tok
    many = side * rows
    pairs = spans // 2
    span = lax.axis_index("span")
    seq = lax.axis_index("seq")
    z_hi = lax.rem(seq, z_far)
    plane = lax.div(seq, z_far)
    row_y, col_x = lax.div(plane, side), lax.rem(plane, side)
    core = lax.rem(span, 2)
    place = z_hi * spans + span
    key_at = jnp.where(core == 0, row_y, col_x)
    query_at = jnp.where(core == 0, col_x, row_y)
    key_step = jnp.where(core == 0, side, 1)
    query_step = jnp.where(core == 0, 1, side)
    my_half = lax.div(place, half_size)

    def at_place(other):
        return {"span": lax.rem(other, spans), "seq": plane * z_far + lax.div(other, spans)}

    def other_place(step):
        half = lax.div(step + 1, 2)
        away = column // 2 + jnp.where(lax.rem(step, 2) == 0, half, -half)
        return lax.rem(place + away, column)

    def key_peer(turn):
        other = lax.rem(key_at + turn, side)
        return {"span": span, "seq": seq + (other - key_at) * key_step * z_far}

    def query_peer(turn):
        other = lax.rem(query_at + turn, side)
        return {"span": span, "seq": seq + (other - query_at) * query_step * z_far}

    def channels(head):
        return pl.ds(pl.multiple_of(head * HEAD_DIM, HEAD_DIM), HEAD_DIM)

    barrier = pltpu.get_barrier_semaphore()

    def greet(step, carry):
        pl.semaphore_signal(barrier, inc=1, device_id=at_place(other_place(step)), device_id_type=MESH)
        return carry

    lax.fori_loop(0, column - 1, greet, 0)
    for turn in range(1, side):
        pl.semaphore_signal(barrier, inc=1, device_id=key_peer(turn), device_id_type=MESH)
        pl.semaphore_signal(barrier, inc=1, device_id=query_peer(turn), device_id_type=MESH)

    arrays = ((key_ref, key_all, 0), (query_ref, query_all, 1), (value_ref, value_all, 2))
    for source, target, n in arrays:
        here = query_at if n == 1 else key_at
        pltpu.make_async_copy(
            source.at[0, :, channels(place)], target.at[here, z_hi, span], recv_sem.at[n, my_half]
        ).start()
    small = [
        pltpu.make_async_copy(counts_ref, counts_s, small_sems.at[0]),
        pltpu.make_async_copy(levels_ref, levels_s, small_sems.at[1]),
        pltpu.make_async_copy(gate_ref.at[:, channels(place)], gate_v, small_sems.at[2]),
    ]
    for copy in small:
        copy.start()
    pl.semaphore_wait(barrier, column - 1 + 2 * (side - 1))

    def zigzag(step):
        half = lax.div(step + 1, 2)
        return jnp.where(lax.rem(step, 2) == 0, half, -half)

    for half in (1, 0):
        first = jnp.where(my_half == half, half_size // 2, 0) + half_size
        for source, target, n in arrays:
            def spread(step, carry, source=source, target=target, n=n, half=half, first=first):
                other = half * half_size + lax.rem(place + first + zigzag(step), half_size)
                along = lax.rem(other, 2) == 0
                there = jnp.where(along, col_x, row_y) if n == 1 else jnp.where(along, row_y, col_x)

                @pl.when(other != place)
                def _():
                    pltpu.make_async_remote_copy(
                        src_ref=source.at[0, :, channels(other)],
                        dst_ref=target.at[there, z_hi, span],
                        send_sem=send_sem.at[n], recv_sem=recv_sem.at[n, my_half],
                        device_id=at_place(other), device_id_type=MESH,
                    ).start()

                return carry
            lax.fori_loop(0, half_size, spread, 0)

    def gather(n, half):
        target = arrays[n][1]
        here, peer = (query_at, query_peer) if n == 1 else (key_at, key_peer)
        sems = (key_sems, query_sems, value_sems)[n]
        block = target.at[here, pl.ds(half * near, near)]
        pltpu.make_async_copy(block, block, recv_sem.at[n, half]).wait()
        copies = []
        for turn in range(1, side):
            copy = pltpu.make_async_remote_copy(
                src_ref=block, dst_ref=block, send_sem=sems.at[0, half, turn],
                recv_sem=sems.at[1, half, turn], device_id=peer(turn), device_id_type=MESH,
            )
            copy.start()
            copies.append(copy)
        return copies

    first = [gather(n, 1) for n in range(3)]
    for copy in small:
        copy.wait()

    block = side * near * tok
    lanes = lax.broadcasted_iota(jnp.int32, (1, 2 * block), 1)
    inside = lax.rem(lanes, block)
    start = plane + (lax.div(inside, near * tok) - key_at) * key_step
    bias = []
    for half in range(2):
        position = start * rows + half * near * tok + lax.rem(inside, near * tok)
        bias.append([
            jnp.where(
                position < jnp.where(lanes < block, counts_s[2 * j], counts_s[2 * j + 1]),
                0.0, MASKED,
            )
            for j in range(pairs)
        ])
    row_ids = lax.broadcasted_iota(jnp.int32, (many, many), 0)
    lane_ids = lax.broadcasted_iota(jnp.int32, (many, many), 1)
    diagonal = row_ids == lane_ids
    row_ids = lax.broadcasted_iota(jnp.int32, (many, 2 * block), 0)
    lane_ids = lax.broadcasted_iota(jnp.int32, (many, 2 * block), 1)
    later = jnp.where((lax.rem(lax.div(row_ids, tok), 2) == 0) & (lane_ids >= block), MASKED, 0.0)
    factor = math.log2(math.e) / math.sqrt(HEAD_DIM)

    def flat(tiles):
        wide = tiles.astype(jnp.float32)
        return wide.reshape(math.prod(wide.shape[:-1]), HEAD_DIM).astype(jnp.bfloat16)

    def flatten(source, target, half):
        for c in range(spans):
            target[half, c * block : (c + 1) * block] = flat(
                source[:, half * near : (half + 1) * near, c]
            )

    def landed(copies):
        for copy in copies:
            copy.wait_recv()

    second = [gather(0, 0), gather(1, 0)]
    landed(first[0])
    flatten(key_all, keys_flat, 1)
    landed(first[2])
    flatten(value_all, values_flat, 1)
    second.append(gather(2, 0))
    landed(first[1])
    landed(second[0])
    flatten(key_all, keys_flat, 0)
    landed(second[1])

    def exchange(source, target, sems, at):
        copies = []
        for turn in range(1, side):
            copy = pltpu.make_async_remote_copy(
                src_ref=source(lax.rem(query_at + turn, side)), dst_ref=target(turn - 1),
                send_sem=sems.at[0, at, turn], recv_sem=sems.at[1, at, turn],
                device_id=query_peer(turn), device_id_type=MESH,
            )
            copy.start()
            copies.append(copy)
        return copies

    def score(half):
        totals = []
        for j in range(pairs):
            wide = 2 * (j + 1) * block
            queries = flat(query_all[:, half * near : (half + 1) * near, 2 * j : 2 * j + 2])
            scores = []
            for part_of in range(2):
                raw = lax.dot_general(
                    queries, keys_flat[part_of, :wide], (((1,), (1,)), ((), ())),
                    preferred_element_type=jnp.float32,
                ) * factor
                for i in range(j + 1):
                    piece = raw[:, 2 * i * block : 2 * (i + 1) * block] + bias[part_of][i]
                    scores.append(piece + later if i == j else piece)
            top = functools.reduce(jnp.maximum, scores)
            top = jnp.maximum(jnp.max(top, axis=1, keepdims=True), LOWEST)
            weights = [jnp.exp2(piece - top) for piece in scores]
            total = jnp.sum(functools.reduce(jnp.add, weights), axis=1, keepdims=True)
            total = jnp.maximum(total, TINY)
            for at, piece in enumerate(weights):
                i = at % (j + 1)
                chances[half, j, at // (j + 1), :, 2 * i * block : 2 * (i + 1) * block] = (
                    piece.astype(jnp.bfloat16)
                )
            both = jnp.sum(jnp.where(diagonal, top + jnp.log2(total), 0.0), axis=0, keepdims=True)
            lse[half, j : j + 1, :] = both
            lse[half, pairs + j : pairs + j + 1, :] = both
            totals.append(1.0 / total)
        return totals, exchange(
            lambda other: lse.at[half], lambda n: lse_in.at[half, n], lse_sems, half
        )

    def weigh(half, j, part_of):
        wide = 2 * (j + 1) * block
        return jnp.dot(
            chances[half, j, part_of, :, :wide], values_flat[part_of, :wide],
            preferred_element_type=jnp.float32,
        )

    scored = [score(0), score(1)]
    for half in range(2):
        for j in range(pairs):
            summed[half, j] = weigh(half, j, 1)
    landed(second[2])
    flatten(value_all, values_flat, 0)

    def mix(half):
        for j in range(pairs):
            mixture = (summed[half, j] + weigh(half, j, 0)) * scored[half][0][j]
            part[half, :, :, 2 * j : 2 * j + 2] = mixture.reshape(
                side, near, 2, tok, HEAD_DIM
            ).astype(jnp.bfloat16)
        return [
            exchange(
                lambda other: part.at[half, other, z], lambda n: part_in.at[half, n, z],
                part_sems, half * near + z,
            )
            for z in range(near)
        ]

    cut = 2 * tok
    row_ids = lax.broadcasted_iota(jnp.int32, (cut, many), 0)
    lane_ids = lax.broadcasted_iota(jnp.int32, (cut, many), 1) - query_at * near * cut

    def share_out(half):
        landed(scored[half][1])
        tables = [lse[half]] + [lse_in[half, n] for n in range(side - 1)]
        top = functools.reduce(jnp.maximum, tables)
        tables = [jnp.exp2(table - top) for table in tables]
        total = functools.reduce(jnp.add, tables)
        tables = [table / total for table in tables]
        return [
            [
                jnp.concatenate([
                    jnp.sum(
                        jnp.where(lane_ids == row_ids + z * cut, table[j : j + 1], 0.0),
                        axis=1, keepdims=True,
                    )
                    for j in range(pairs)
                ], axis=0)
                for table in tables
            ]
            for z in range(near)
        ]

    parts = mix(0)
    shares = share_out(0)
    gates = jnp.concatenate([
        jnp.broadcast_to(gate_v[pl.ds(levels_s[i], 1), :], (tok, HEAD_DIM)) for i in range(spans)
    ], axis=0)
    parts += mix(1)
    shares += share_out(1)

    for level in range(z_far):
        half, z = level // near, level % near
        landed(parts[level])
        attended = jnp.zeros((spans * tok, HEAD_DIM), jnp.float32)
        for n in range(side):
            tile = part[half, query_at, z] if n == 0 else part_in[half, n - 1, z]
            tile = tile.astype(jnp.float32).reshape(spans * tok, HEAD_DIM)
            attended = attended + shares[level][n] * tile
        mean = jnp.mean(attended * attended, axis=1, keepdims=True)
        normed = attended * lax.rsqrt(mean + EPSILON) * gates
        mixed[level] = normed.reshape(spans, tok, HEAD_DIM).astype(jnp.bfloat16)

        def send_back(step, carry, level=level):
            other_span = lax.rem(span + step, spans)
            other = level * spans + other_span

            @pl.when(other != place)
            def _():
                pltpu.make_async_remote_copy(
                    src_ref=mixed.at[level, other_span],
                    dst_ref=out_ref.at[0, :, channels(place)],
                    send_sem=out_send, recv_sem=out_recv,
                    device_id=at_place(other), device_id_type=MESH,
                ).start()

            @pl.when(other == place)
            def _():
                pltpu.make_async_copy(
                    mixed.at[level, other_span], out_ref.at[0, :, channels(place)], out_recv
                ).start()

            return carry

        lax.fori_loop(0, spans, send_back, 0)

    sent = [copy for group in first + second + parts for copy in group]
    sent += scored[0][1] + scored[1][1]
    for source, target, n in arrays:
        rest = source.at[0, :, pl.ds(0, (column - 1) * HEAD_DIM)]
        pltpu.make_async_copy(rest, rest, send_sem.at[n]).wait()
    for copy in sent:
        copy.wait_send()
    rest = out_ref.at[0, :, pl.ds(0, (column - 1) * HEAD_DIM)]
    pltpu.make_async_copy(rest, rest, out_send).wait()
    pltpu.make_async_copy(out_ref, out_ref, out_recv).wait()


def body(query_rows, key_rows, value_rows, counts, levels, gate_table):
    spans = lax.axis_size("span")
    seq_size = lax.axis_size("seq")
    tok, width = query_rows.shape[1:]
    column = width // HEAD_DIM
    z_far = column // spans
    side = math.isqrt(seq_size // z_far)
    many = side * z_far * tok
    pairs = spans // 2
    bf16, f32 = jnp.bfloat16, jnp.float32
    gathered = pltpu.VMEM((side, z_far, spans, tok, HEAD_DIM), bf16)
    flat = pltpu.VMEM((2, spans * many // 2, HEAD_DIM), bf16)
    dma = pltpu.SemaphoreType.DMA
    hbm = pl.BlockSpec(memory_space=pltpu.HBM)
    return pl.pallas_call(
        functools.partial(kernel, spans, z_far, side, tok),
        out_shape=jax.ShapeDtypeStruct(query_rows.shape, bf16),
        in_specs=[hbm] * 6,
        out_specs=pl.BlockSpec(memory_space=pl.ANY),
        scratch_shapes=[
            gathered, gathered, gathered, flat, flat,
            pltpu.VMEM((2, pairs, 2, many, spans * many // 2), bf16),
            pltpu.VMEM((2, pairs, many, HEAD_DIM), f32),
            pltpu.VMEM((2, side, z_far // 2, spans, tok, HEAD_DIM), bf16),
            pltpu.VMEM((2, side - 1, z_far // 2, spans, tok, HEAD_DIM), bf16),
            pltpu.VMEM((2, 2 * pairs, many), f32),
            pltpu.VMEM((2, side - 1, 2 * pairs, many), f32),
            pltpu.VMEM((z_far, spans, tok, HEAD_DIM), bf16),
            pltpu.VMEM((gate_table.shape[0], HEAD_DIM), f32),
            pltpu.SMEM(counts.shape, jnp.int32),
            pltpu.SMEM(levels.shape, jnp.int32),
            dma((3,)), dma((3, 2)),
            dma((2, 2, side)), dma((2, 2, side)), dma((2, 2, side)),
            dma((2, z_far, side)), dma((2, 2, side)),
            dma, dma, dma((3,)),
        ],
        compiler_params=pltpu.CompilerParams(
            collective_id=0, has_side_effects=True, vmem_limit_bytes=VMEM_BYTES
        ),
        cost_estimate=pl.CostEstimate(
            flops=600_000_000, bytes_accessed=1_000_000, transcendentals=700_000
        ),
    )(*[
        pltpu.with_memory_space_constraint(array, pltpu.HBM)
        for array in (query_rows, key_rows, value_rows, counts, levels, gate_table)
    ])


def solution(mesh):
    placed = (P("span", "seq", None), P("span", "seq", None), P("span", "seq", None), P(), P(), P())
    return jax.shard_map(
        body, mesh=mesh, in_specs=placed, out_specs=P("span", "seq", None), check_vma=False
    )
```

```python
import functools
import math

import jax
import jax.numpy as jnp
from jax import lax
from jax.experimental import pallas as pl
from jax.experimental.pallas import tpu as pltpu
from jax.sharding import PartitionSpec as P

HEAD_DIM = 128
EPSILON = 1e-5
MASKED = -1e30
LOWEST = -1e4
TINY = 1e-30
MESH = pl.DeviceIdType.MESH
VMEM_BYTES = 32 * 1024 * 1024


def kernel(
    spans, z_far, side, tok,
    query_ref, key_ref, value_ref, counts_ref, levels_ref, gate_ref, out_ref,
    key_all, query_all, value_all, keys_flat, values_flat, chances, summed, part, part_in, lse, lse_in,
    mixed, gate_v, counts_s, levels_s,
    send_sem, recv_sem, key_sems, query_sems, value_sems, part_sems, lse_sems,
    out_send, out_recv, small_sems,
):
    column = spans * z_far
    half_size = column // 2
    near = z_far // 2
    rows = z_far * tok
    many = side * rows
    pairs = spans // 2
    span = lax.axis_index("span")
    seq = lax.axis_index("seq")
    z_hi = lax.rem(seq, z_far)
    plane = lax.div(seq, z_far)
    row_y, col_x = lax.div(plane, side), lax.rem(plane, side)
    core = lax.rem(span, 2)
    place = z_hi * spans + span
    key_at = jnp.where(core == 0, row_y, col_x)
    query_at = jnp.where(core == 0, col_x, row_y)
    key_step = jnp.where(core == 0, side, 1)
    query_step = jnp.where(core == 0, 1, side)
    my_half = lax.div(place, half_size)

    def at_place(other):
        return {"span": lax.rem(other, spans), "seq": plane * z_far + lax.div(other, spans)}

    def other_place(step):
        half = lax.div(step + 1, 2)
        away = column // 2 + jnp.where(lax.rem(step, 2) == 0, half, -half)
        return lax.rem(place + away, column)

    def key_peer(turn):
        other = lax.rem(key_at + turn, side)
        return {"span": span, "seq": seq + (other - key_at) * key_step * z_far}

    def query_peer(turn):
        other = lax.rem(query_at + turn, side)
        return {"span": span, "seq": seq + (other - query_at) * query_step * z_far}

    def channels(head):
        return pl.ds(pl.multiple_of(head * HEAD_DIM, HEAD_DIM), HEAD_DIM)

    barrier = pltpu.get_barrier_semaphore()

    def greet(step, carry):
        pl.semaphore_signal(barrier, inc=1, device_id=at_place(other_place(step)), device_id_type=MESH)
        return carry

    lax.fori_loop(0, column - 1, greet, 0)
    for turn in range(1, side):
        pl.semaphore_signal(barrier, inc=1, device_id=key_peer(turn), device_id_type=MESH)
        pl.semaphore_signal(barrier, inc=1, device_id=query_peer(turn), device_id_type=MESH)

    arrays = ((key_ref, key_all, 0), (query_ref, query_all, 1), (value_ref, value_all, 2))
    for source, target, n in arrays:
        here = query_at if n == 1 else key_at
        pltpu.make_async_copy(
            source.at[0, :, channels(place)], target.at[here, z_hi, span], recv_sem.at[n, my_half]
        ).start()
    small = [
        pltpu.make_async_copy(counts_ref, counts_s, small_sems.at[0]),
        pltpu.make_async_copy(levels_ref, levels_s, small_sems.at[1]),
        pltpu.make_async_copy(gate_ref.at[:, channels(place)], gate_v, small_sems.at[2]),
    ]
    for copy in small:
        copy.start()
    pl.semaphore_wait(barrier, column - 1 + 2 * (side - 1))

    def zigzag(step):
        half = lax.div(step + 1, 2)
        return jnp.where(lax.rem(step, 2) == 0, half, -half)

    for source, target, n in arrays:
        def spread(step, carry, source=source, target=target, n=n):
            other = other_place(step)
            along = lax.rem(other, 2) == 0
            there = jnp.where(along, col_x, row_y) if n == 1 else jnp.where(along, row_y, col_x)
            pltpu.make_async_remote_copy(
                src_ref=source.at[0, :, channels(other)], dst_ref=target.at[there, z_hi, span],
                send_sem=send_sem.at[n], recv_sem=recv_sem.at[n, my_half],
                device_id=at_place(other), device_id_type=MESH,
            ).start()
            return carry
        lax.fori_loop(0, column - 1, spread, 0)

    def gather(n, half):
        target = arrays[n][1]
        here, peer = (query_at, query_peer) if n == 1 else (key_at, key_peer)
        sems = (key_sems, query_sems, value_sems)[n]
        block = target.at[here, pl.ds(half * near, near)]
        pltpu.make_async_copy(block, block, recv_sem.at[n, half]).wait()
        copies = []
        for turn in range(1, side):
            copy = pltpu.make_async_remote_copy(
                src_ref=block, dst_ref=block, send_sem=sems.at[0, half, turn],
                recv_sem=sems.at[1, half, turn], device_id=peer(turn), device_id_type=MESH,
            )
            copy.start()
            copies.append(copy)
        return copies

    first = [gather(0, 1), gather(1, 1)]
    second = [gather(0, 0), gather(1, 0)]
    first.append(gather(2, 1))
    second.append(gather(2, 0))
    for copy in small:
        copy.wait()

    block = side * near * tok
    lanes = lax.broadcasted_iota(jnp.int32, (1, 2 * block), 1)
    inside = lax.rem(lanes, block)
    start = plane + (lax.div(inside, near * tok) - key_at) * key_step
    bias = []
    for half in range(2):
        position = start * rows + half * near * tok + lax.rem(inside, near * tok)
        bias.append([
            jnp.where(
                position < jnp.where(lanes < block, counts_s[2 * j], counts_s[2 * j + 1]),
                0.0, MASKED,
            )
            for j in range(pairs)
        ])
    row_ids = lax.broadcasted_iota(jnp.int32, (many, many), 0)
    lane_ids = lax.broadcasted_iota(jnp.int32, (many, many), 1)
    diagonal = row_ids == lane_ids
    row_ids = lax.broadcasted_iota(jnp.int32, (many, 2 * block), 0)
    lane_ids = lax.broadcasted_iota(jnp.int32, (many, 2 * block), 1)
    later = jnp.where((lax.rem(lax.div(row_ids, tok), 2) == 0) & (lane_ids >= block), MASKED, 0.0)
    factor = math.log2(math.e) / math.sqrt(HEAD_DIM)

    def flat(tiles):
        wide = tiles.astype(jnp.float32)
        return wide.reshape(math.prod(wide.shape[:-1]), HEAD_DIM).astype(jnp.bfloat16)

    def flatten(source, target, half):
        for c in range(spans):
            target[half, c * block : (c + 1) * block] = flat(
                source[:, half * near : (half + 1) * near, c]
            )

    def landed(copies):
        for copy in copies:
            copy.wait_recv()

    landed(first[0])
    flatten(key_all, keys_flat, 1)
    landed(first[2])
    flatten(value_all, values_flat, 1)
    landed(first[1])
    landed(second[0])
    flatten(key_all, keys_flat, 0)
    landed(second[1])

    def exchange(source, target, sems, at):
        copies = []
        for turn in range(1, side):
            copy = pltpu.make_async_remote_copy(
                src_ref=source(lax.rem(query_at + turn, side)), dst_ref=target(turn - 1),
                send_sem=sems.at[0, at, turn], recv_sem=sems.at[1, at, turn],
                device_id=query_peer(turn), device_id_type=MESH,
            )
            copy.start()
            copies.append(copy)
        return copies

    def score(half):
        totals = []
        for j in range(pairs):
            wide = 2 * (j + 1) * block
            queries = flat(query_all[:, half * near : (half + 1) * near, 2 * j : 2 * j + 2])
            scores = []
            for part_of in range(2):
                raw = lax.dot_general(
                    queries, keys_flat[part_of, :wide], (((1,), (1,)), ((), ())),
                    preferred_element_type=jnp.float32,
                ) * factor
                for i in range(j + 1):
                    piece = raw[:, 2 * i * block : 2 * (i + 1) * block] + bias[part_of][i]
                    scores.append(piece + later if i == j else piece)
            top = functools.reduce(jnp.maximum, scores)
            top = jnp.maximum(jnp.max(top, axis=1, keepdims=True), LOWEST)
            weights = [jnp.exp2(piece - top) for piece in scores]
            total = jnp.sum(functools.reduce(jnp.add, weights), axis=1, keepdims=True)
            total = jnp.maximum(total, TINY)
            for at, piece in enumerate(weights):
                i = at % (j + 1)
                chances[half, j, at // (j + 1), :, 2 * i * block : 2 * (i + 1) * block] = (
                    piece.astype(jnp.bfloat16)
                )
            both = jnp.sum(jnp.where(diagonal, top + jnp.log2(total), 0.0), axis=0, keepdims=True)
            lse[half, j : j + 1, :] = both
            lse[half, pairs + j : pairs + j + 1, :] = both
            totals.append(1.0 / total)
        return totals, exchange(
            lambda other: lse.at[half], lambda n: lse_in.at[half, n], lse_sems, half
        )

    def weigh(half, j, part_of):
        wide = 2 * (j + 1) * block
        return jnp.dot(
            chances[half, j, part_of, :, :wide], values_flat[part_of, :wide],
            preferred_element_type=jnp.float32,
        )

    scored = [score(0), score(1)]
    for half in range(2):
        for j in range(pairs):
            summed[half, j] = weigh(half, j, 1)
    landed(second[2])
    flatten(value_all, values_flat, 0)

    def mix(half):
        for j in range(pairs):
            mixture = (summed[half, j] + weigh(half, j, 0)) * scored[half][0][j]
            part[half, :, :, 2 * j : 2 * j + 2] = mixture.reshape(
                side, near, 2, tok, HEAD_DIM
            ).astype(jnp.bfloat16)
        return [
            exchange(
                lambda other: part.at[half, other, z], lambda n: part_in.at[half, n, z],
                part_sems, half * near + z,
            )
            for z in range(near)
        ]

    cut = 2 * tok
    row_ids = lax.broadcasted_iota(jnp.int32, (cut, many), 0)
    lane_ids = lax.broadcasted_iota(jnp.int32, (cut, many), 1) - query_at * near * cut

    def share_out(half):
        landed(scored[half][1])
        tables = [lse[half]] + [lse_in[half, n] for n in range(side - 1)]
        top = functools.reduce(jnp.maximum, tables)
        tables = [jnp.exp2(table - top) for table in tables]
        total = functools.reduce(jnp.add, tables)
        tables = [table / total for table in tables]
        return [
            [
                jnp.concatenate([
                    jnp.sum(
                        jnp.where(lane_ids == row_ids + z * cut, table[j : j + 1], 0.0),
                        axis=1, keepdims=True,
                    )
                    for j in range(pairs)
                ], axis=0)
                for table in tables
            ]
            for z in range(near)
        ]

    parts = mix(0)
    shares = share_out(0)
    gates = jnp.concatenate([
        jnp.broadcast_to(gate_v[pl.ds(levels_s[i], 1), :], (tok, HEAD_DIM)) for i in range(spans)
    ], axis=0)
    parts += mix(1)
    shares += share_out(1)

    for level in range(z_far):
        half, z = level // near, level % near
        landed(parts[level])
        attended = jnp.zeros((spans * tok, HEAD_DIM), jnp.float32)
        for n in range(side):
            tile = part[half, query_at, z] if n == 0 else part_in[half, n - 1, z]
            tile = tile.astype(jnp.float32).reshape(spans * tok, HEAD_DIM)
            attended = attended + shares[level][n] * tile
        mean = jnp.mean(attended * attended, axis=1, keepdims=True)
        normed = attended * lax.rsqrt(mean + EPSILON) * gates
        mixed[level] = normed.reshape(spans, tok, HEAD_DIM).astype(jnp.bfloat16)

        def send_back(step, carry, level=level):
            other_span = step
            other = level * spans + other_span

            @pl.when(other != place)
            def _():
                pltpu.make_async_remote_copy(
                    src_ref=mixed.at[level, other_span],
                    dst_ref=out_ref.at[0, :, channels(place)],
                    send_sem=out_send, recv_sem=out_recv,
                    device_id=at_place(other), device_id_type=MESH,
                ).start()

            @pl.when(other == place)
            def _():
                pltpu.make_async_copy(
                    mixed.at[level, other_span], out_ref.at[0, :, channels(place)], out_recv
                ).start()

            return carry

        lax.fori_loop(0, spans, send_back, 0)

    sent = [copy for group in first + second + parts for copy in group]
    sent += scored[0][1] + scored[1][1]
    for source, target, n in arrays:
        rest = source.at[0, :, pl.ds(0, (column - 1) * HEAD_DIM)]
        pltpu.make_async_copy(rest, rest, send_sem.at[n]).wait()
    for copy in sent:
        copy.wait_send()
    rest = out_ref.at[0, :, pl.ds(0, (column - 1) * HEAD_DIM)]
    pltpu.make_async_copy(rest, rest, out_send).wait()
    pltpu.make_async_copy(out_ref, out_ref, out_recv).wait()


def body(query_rows, key_rows, value_rows, counts, levels, gate_table):
    spans = lax.axis_size("span")
    seq_size = lax.axis_size("seq")
    tok, width = query_rows.shape[1:]
    column = width // HEAD_DIM
    z_far = column // spans
    side = math.isqrt(seq_size // z_far)
    many = side * z_far * tok
    pairs = spans // 2
    bf16, f32 = jnp.bfloat16, jnp.float32
    gathered = pltpu.VMEM((side, z_far, spans, tok, HEAD_DIM), bf16)
    flat = pltpu.VMEM((2, spans * many // 2, HEAD_DIM), bf16)
    dma = pltpu.SemaphoreType.DMA
    hbm = pl.BlockSpec(memory_space=pltpu.HBM)
    return pl.pallas_call(
        functools.partial(kernel, spans, z_far, side, tok),
        out_shape=jax.ShapeDtypeStruct(query_rows.shape, bf16),
        in_specs=[hbm] * 6,
        out_specs=pl.BlockSpec(memory_space=pl.ANY),
        scratch_shapes=[
            gathered, gathered, gathered, flat, flat,
            pltpu.VMEM((2, pairs, 2, many, spans * many // 2), bf16),
            pltpu.VMEM((2, pairs, many, HEAD_DIM), f32),
            pltpu.VMEM((2, side, z_far // 2, spans, tok, HEAD_DIM), bf16),
            pltpu.VMEM((2, side - 1, z_far // 2, spans, tok, HEAD_DIM), bf16),
            pltpu.VMEM((2, 2 * pairs, many), f32),
            pltpu.VMEM((2, side - 1, 2 * pairs, many), f32),
            pltpu.VMEM((z_far, spans, tok, HEAD_DIM), bf16),
            pltpu.VMEM((gate_table.shape[0], HEAD_DIM), f32),
            pltpu.SMEM(counts.shape, jnp.int32),
            pltpu.SMEM(levels.shape, jnp.int32),
            dma((3,)), dma((3, 2)),
            dma((2, 2, side)), dma((2, 2, side)), dma((2, 2, side)),
            dma((2, z_far, side)), dma((2, 2, side)),
            dma, dma, dma((3,)),
        ],
        compiler_params=pltpu.CompilerParams(
            collective_id=0, has_side_effects=True, vmem_limit_bytes=VMEM_BYTES
        ),
        cost_estimate=pl.CostEstimate(
            flops=600_000_000, bytes_accessed=1_000_000, transcendentals=700_000
        ),
    )(*[
        pltpu.with_memory_space_constraint(array, pltpu.HBM)
        for array in (query_rows, key_rows, value_rows, counts, levels, gate_table)
    ])


def solution(mesh):
    placed = (P("span", "seq", None), P("span", "seq", None), P("span", "seq", None), P(), P(), P())
    return jax.shard_map(
        body, mesh=mesh, in_specs=placed, out_specs=P("span", "seq", None), check_vma=False
    )
```

```python
import functools
import math

import jax
import jax.numpy as jnp
from jax import lax
from jax.experimental import pallas as pl
from jax.experimental.pallas import tpu as pltpu
from jax.sharding import PartitionSpec as P

HEAD_DIM = 128
EPSILON = 1e-5
MASKED = -1e30
LOWEST = -1e4
TINY = 1e-30
MESH = pl.DeviceIdType.MESH
VMEM_BYTES = 32 * 1024 * 1024


def kernel(
    spans, z_far, side, tok,
    query_ref, key_ref, value_ref, counts_ref, levels_ref, gate_ref, out_ref,
    key_rows, query_rows, paired, paired_in, key_all, query_all, value_all, keys_flat, values_flat, chances, summed, part, part_in, lse, lse_in,
    mixed, gate_v, counts_s, levels_s,
    load_sems, send_sem, recv_sem, key_sems, query_sems, value_sems, part_sems, lse_sems,
    out_send, out_recv, small_sems,
):
    column = spans * z_far
    half_size = column // 2
    near = z_far // 2
    rows = z_far * tok
    many = side * rows
    pairs = spans // 2
    span = lax.axis_index("span")
    seq = lax.axis_index("seq")
    z_hi = lax.rem(seq, z_far)
    plane = lax.div(seq, z_far)
    row_y, col_x = lax.div(plane, side), lax.rem(plane, side)
    core = lax.rem(span, 2)
    place = z_hi * spans + span
    key_at = jnp.where(core == 0, row_y, col_x)
    query_at = jnp.where(core == 0, col_x, row_y)
    key_step = jnp.where(core == 0, side, 1)
    query_step = jnp.where(core == 0, 1, side)
    my_half = lax.div(place, half_size)

    def at_place(other):
        return {"span": lax.rem(other, spans), "seq": plane * z_far + lax.div(other, spans)}

    def other_place(step):
        half = lax.div(step + 1, 2)
        away = column // 2 + jnp.where(lax.rem(step, 2) == 0, half, -half)
        return lax.rem(place + away, column)

    def key_peer(turn):
        other = lax.rem(key_at + turn, side)
        return {"span": span, "seq": seq + (other - key_at) * key_step * z_far}

    def query_peer(turn):
        other = lax.rem(query_at + turn, side)
        return {"span": span, "seq": seq + (other - query_at) * query_step * z_far}

    def channels(head):
        return pl.ds(pl.multiple_of(head * HEAD_DIM, HEAD_DIM), HEAD_DIM)

    barrier = pltpu.get_barrier_semaphore()

    def greet(step, carry):
        pl.semaphore_signal(barrier, inc=1, device_id=at_place(other_place(step)), device_id_type=MESH)
        return carry

    lax.fori_loop(0, column - 1, greet, 0)
    for turn in range(1, side):
        pl.semaphore_signal(barrier, inc=1, device_id=key_peer(turn), device_id_type=MESH)
        pl.semaphore_signal(barrier, inc=1, device_id=query_peer(turn), device_id_type=MESH)

    loads = []
    for n, (source, target) in enumerate(((key_ref, key_rows), (query_ref, query_rows))):
        copy = pltpu.make_async_copy(source, target, load_sems.at[n])
        copy.start()
        loads.append(copy)
    pltpu.make_async_copy(
        value_ref.at[0, :, channels(place)], value_all.at[key_at, z_hi, span], recv_sem.at[1, my_half]
    ).start()
    small = [
        pltpu.make_async_copy(counts_ref, counts_s, small_sems.at[0]),
        pltpu.make_async_copy(levels_ref, levels_s, small_sems.at[1]),
        pltpu.make_async_copy(gate_ref.at[:, channels(place)], gate_v, small_sems.at[2]),
    ]
    for copy in small:
        copy.start()
    for n, source in enumerate((key_rows, query_rows)):
        loads[n].wait()
        for head in range(column):
            paired[head, n] = source[0, :, head * HEAD_DIM : (head + 1) * HEAD_DIM]
    pltpu.make_async_copy(
        paired.at[place], paired_in.at[z_hi, span], recv_sem.at[0, my_half]
    ).start()
    pl.semaphore_wait(barrier, column - 1 + 2 * (side - 1))

    def spread_pairs(step, carry):
        other = other_place(step)
        pltpu.make_async_remote_copy(
            src_ref=paired.at[other], dst_ref=paired_in.at[z_hi, span],
            send_sem=send_sem.at[0], recv_sem=recv_sem.at[0, my_half],
            device_id=at_place(other), device_id_type=MESH,
        ).start()
        return carry

    def spread_values(step, carry):
        other = other_place(step)
        there = jnp.where(lax.rem(other, 2) == 0, row_y, col_x)
        pltpu.make_async_remote_copy(
            src_ref=value_ref.at[0, :, channels(other)], dst_ref=value_all.at[there, z_hi, span],
            send_sem=send_sem.at[1], recv_sem=recv_sem.at[1, my_half],
            device_id=at_place(other), device_id_type=MESH,
        ).start()
        return carry

    lax.fori_loop(0, column - 1, spread_pairs, 0)
    lax.fori_loop(0, column - 1, spread_values, 0)

    def gather(n, half):
        target, sems = ((key_all, key_sems), (query_all, query_sems), (value_all, value_sems))[n]
        here, peer = (query_at, query_peer) if n == 1 else (key_at, key_peer)
        slab = pl.ds(half * near, near)
        block = target.at[here, slab]
        source = block if n == 2 else paired_in.at[slab, :, n]
        copies = []
        for turn in range(1, side):
            copy = pltpu.make_async_remote_copy(
                src_ref=source, dst_ref=block, send_sem=sems.at[0, half, turn],
                recv_sem=sems.at[1, half, turn], device_id=peer(turn), device_id_type=MESH,
            )
            copy.start()
            copies.append(copy)
        if n < 2:
            target[here, half * near : (half + 1) * near] = paired_in[
                half * near : (half + 1) * near, :, n
            ]
        return copies

    def arrive(target, n, half):
        block = target.at[pl.ds(half * near, near)]
        pltpu.make_async_copy(block, block, recv_sem.at[n, half]).wait()

    first, second = [], []
    for half, copies in ((1, first), (0, second)):
        arrive(paired_in, 0, half)
        copies.append(gather(0, half))
        copies.append(gather(1, half))
    for half, copies in ((1, first), (0, second)):
        arrive(value_all.at[key_at], 1, half)
        copies.append(gather(2, half))
    for copy in small:
        copy.wait()

    block = side * near * tok
    lanes = lax.broadcasted_iota(jnp.int32, (1, 2 * block), 1)
    inside = lax.rem(lanes, block)
    start = plane + (lax.div(inside, near * tok) - key_at) * key_step
    bias = []
    for half in range(2):
        position = start * rows + half * near * tok + lax.rem(inside, near * tok)
        bias.append([
            jnp.where(
                position < jnp.where(lanes < block, counts_s[2 * j], counts_s[2 * j + 1]),
                0.0, MASKED,
            )
            for j in range(pairs)
        ])
    row_ids = lax.broadcasted_iota(jnp.int32, (many, many), 0)
    lane_ids = lax.broadcasted_iota(jnp.int32, (many, many), 1)
    diagonal = row_ids == lane_ids
    row_ids = lax.broadcasted_iota(jnp.int32, (many, 2 * block), 0)
    lane_ids = lax.broadcasted_iota(jnp.int32, (many, 2 * block), 1)
    later = jnp.where((lax.rem(lax.div(row_ids, tok), 2) == 0) & (lane_ids >= block), MASKED, 0.0)
    factor = math.log2(math.e) / math.sqrt(HEAD_DIM)

    def flat(tiles):
        wide = tiles.astype(jnp.float32)
        return wide.reshape(math.prod(wide.shape[:-1]), HEAD_DIM).astype(jnp.bfloat16)

    def flatten(source, target, half):
        for c in range(spans):
            target[half, c * block : (c + 1) * block] = flat(
                source[:, half * near : (half + 1) * near, c]
            )

    def landed(copies):
        for copy in copies:
            copy.wait_recv()

    landed(first[0])
    flatten(key_all, keys_flat, 1)
    landed(first[2])
    flatten(value_all, values_flat, 1)
    landed(first[1])
    landed(second[0])
    flatten(key_all, keys_flat, 0)
    landed(second[1])

    def exchange(source, target, sems, at):
        copies = []
        for turn in range(1, side):
            copy = pltpu.make_async_remote_copy(
                src_ref=source(lax.rem(query_at + turn, side)), dst_ref=target(turn - 1),
                send_sem=sems.at[0, at, turn], recv_sem=sems.at[1, at, turn],
                device_id=query_peer(turn), device_id_type=MESH,
            )
            copy.start()
            copies.append(copy)
        return copies

    def score(half):
        totals = []
        for j in range(pairs):
            wide = 2 * (j + 1) * block
            queries = flat(query_all[:, half * near : (half + 1) * near, 2 * j : 2 * j + 2])
            scores = []
            for part_of in range(2):
                raw = lax.dot_general(
                    queries, keys_flat[part_of, :wide], (((1,), (1,)), ((), ())),
                    preferred_element_type=jnp.float32,
                ) * factor
                for i in range(j + 1):
                    piece = raw[:, 2 * i * block : 2 * (i + 1) * block] + bias[part_of][i]
                    scores.append(piece + later if i == j else piece)
            top = functools.reduce(jnp.maximum, scores)
            top = jnp.maximum(jnp.max(top, axis=1, keepdims=True), LOWEST)
            weights = [jnp.exp2(piece - top) for piece in scores]
            total = jnp.sum(functools.reduce(jnp.add, weights), axis=1, keepdims=True)
            total = jnp.maximum(total, TINY)
            for at, piece in enumerate(weights):
                i = at % (j + 1)
                chances[half, j, at // (j + 1), :, 2 * i * block : 2 * (i + 1) * block] = (
                    piece.astype(jnp.bfloat16)
                )
            both = jnp.sum(jnp.where(diagonal, top + jnp.log2(total), 0.0), axis=0, keepdims=True)
            lse[half, j : j + 1, :] = both
            totals.append(1.0 / total)
        return totals, exchange(
            lambda other: lse.at[half], lambda n: lse_in.at[half, n], lse_sems, half
        )

    def weigh(half, j, part_of):
        wide = 2 * (j + 1) * block
        return jnp.dot(
            chances[half, j, part_of, :, :wide], values_flat[part_of, :wide],
            preferred_element_type=jnp.float32,
        )

    scored = [score(0), score(1)]
    for half in range(2):
        for j in range(pairs):
            summed[half, j] = weigh(half, j, 1)
    landed(second[2])
    flatten(value_all, values_flat, 0)

    def mix(half):
        for j in range(pairs):
            mixture = (summed[half, j] + weigh(half, j, 0)) * scored[half][0][j]
            part[half, :, :, 2 * j : 2 * j + 2] = mixture.reshape(
                side, near, 2, tok, HEAD_DIM
            ).astype(jnp.bfloat16)
        return [
            exchange(
                lambda other: part.at[half, other, z], lambda n: part_in.at[half, n, z],
                part_sems, half * near + z,
            )
            for z in range(near)
        ]

    cut = 2 * tok
    row_ids = lax.broadcasted_iota(jnp.int32, (cut, many), 0)
    lane_ids = lax.broadcasted_iota(jnp.int32, (cut, many), 1) - query_at * near * cut

    def share_out(half):
        landed(scored[half][1])
        tables = [lse[half]] + [lse_in[half, n] for n in range(side - 1)]
        top = functools.reduce(jnp.maximum, tables)
        tables = [jnp.exp2(table - top) for table in tables]
        total = functools.reduce(jnp.add, tables)
        tables = [table / total for table in tables]
        return [
            [
                jnp.concatenate([
                    jnp.sum(
                        jnp.where(lane_ids == row_ids + z * cut, table[j : j + 1], 0.0),
                        axis=1, keepdims=True,
                    )
                    for j in range(pairs)
                ], axis=0)
                for table in tables
            ]
            for z in range(near)
        ]

    parts = mix(0)
    shares = share_out(0)
    gates = jnp.concatenate([
        jnp.broadcast_to(gate_v[pl.ds(levels_s[i], 1), :], (tok, HEAD_DIM)) for i in range(spans)
    ], axis=0)
    parts += mix(1)
    shares += share_out(1)

    for level in range(z_far):
        half, z = level // near, level % near
        landed(parts[level])
        attended = jnp.zeros((spans * tok, HEAD_DIM), jnp.float32)
        for n in range(side):
            tile = part[half, query_at, z] if n == 0 else part_in[half, n - 1, z]
            tile = tile.astype(jnp.float32).reshape(spans * tok, HEAD_DIM)
            attended = attended + shares[level][n] * tile
        mean = jnp.mean(attended * attended, axis=1, keepdims=True)
        normed = attended * lax.rsqrt(mean + EPSILON) * gates
        mixed[level] = normed.reshape(spans, tok, HEAD_DIM).astype(jnp.bfloat16)

        def send_back(step, carry, level=level):
            other_span = step
            other = level * spans + other_span

            @pl.when(other != place)
            def _():
                pltpu.make_async_remote_copy(
                    src_ref=mixed.at[level, other_span],
                    dst_ref=out_ref.at[0, :, channels(place)],
                    send_sem=out_send, recv_sem=out_recv,
                    device_id=at_place(other), device_id_type=MESH,
                ).start()

            @pl.when(other == place)
            def _():
                pltpu.make_async_copy(
                    mixed.at[level, other_span], out_ref.at[0, :, channels(place)], out_recv
                ).start()

            return carry

        lax.fori_loop(0, spans, send_back, 0)

    sent = [copy for group in first + second + parts for copy in group]
    sent += scored[0][1] + scored[1][1]
    rest = paired.at[pl.ds(0, column - 1)]
    pltpu.make_async_copy(rest, rest, send_sem.at[0]).wait()
    rest = value_ref.at[0, :, pl.ds(0, (column - 1) * HEAD_DIM)]
    pltpu.make_async_copy(rest, rest, send_sem.at[1]).wait()
    for copy in sent:
        copy.wait_send()
    rest = out_ref.at[0, :, pl.ds(0, (column - 1) * HEAD_DIM)]
    pltpu.make_async_copy(rest, rest, out_send).wait()
    pltpu.make_async_copy(out_ref, out_ref, out_recv).wait()


def body(query_rows, key_rows, value_rows, counts, levels, gate_table):
    spans = lax.axis_size("span")
    seq_size = lax.axis_size("seq")
    tok, width = query_rows.shape[1:]
    column = width // HEAD_DIM
    z_far = column // spans
    side = math.isqrt(seq_size // z_far)
    many = side * z_far * tok
    pairs = spans // 2
    bf16, f32 = jnp.bfloat16, jnp.float32
    gathered = pltpu.VMEM((side, z_far, spans, tok, HEAD_DIM), bf16)
    flat = pltpu.VMEM((2, spans * many // 2, HEAD_DIM), bf16)
    dma = pltpu.SemaphoreType.DMA
    hbm = pl.BlockSpec(memory_space=pltpu.HBM)
    return pl.pallas_call(
        functools.partial(kernel, spans, z_far, side, tok),
        out_shape=jax.ShapeDtypeStruct(query_rows.shape, bf16),
        in_specs=[hbm] * 6,
        out_specs=pl.BlockSpec(memory_space=pl.ANY),
        scratch_shapes=[
            pltpu.VMEM(key_rows.shape, bf16),
            pltpu.VMEM(query_rows.shape, bf16),
            pltpu.VMEM((column, 2, tok, HEAD_DIM), bf16),
            pltpu.VMEM((z_far, spans, 2, tok, HEAD_DIM), bf16),
            gathered, gathered, gathered, flat, flat,
            pltpu.VMEM((2, pairs, 2, many, spans * many // 2), bf16),
            pltpu.VMEM((2, pairs, many, HEAD_DIM), f32),
            pltpu.VMEM((2, side, z_far // 2, spans, tok, HEAD_DIM), bf16),
            pltpu.VMEM((2, side - 1, z_far // 2, spans, tok, HEAD_DIM), bf16),
            pltpu.VMEM((2, pairs, many), f32),
            pltpu.VMEM((2, side - 1, pairs, many), f32),
            pltpu.VMEM((z_far, spans, tok, HEAD_DIM), bf16),
            pltpu.VMEM((gate_table.shape[0], HEAD_DIM), f32),
            pltpu.SMEM(counts.shape, jnp.int32),
            pltpu.SMEM(levels.shape, jnp.int32),
            dma((2,)), dma((2,)), dma((2, 2)),
            dma((2, 2, side)), dma((2, 2, side)), dma((2, 2, side)),
            dma((2, z_far, side)), dma((2, 2, side)),
            dma, dma, dma((3,)),
        ],
        compiler_params=pltpu.CompilerParams(
            collective_id=0, has_side_effects=True, vmem_limit_bytes=VMEM_BYTES
        ),
        cost_estimate=pl.CostEstimate(
            flops=600_000_000, bytes_accessed=1_000_000, transcendentals=700_000
        ),
    )(*[
        pltpu.with_memory_space_constraint(array, pltpu.HBM)
        for array in (query_rows, key_rows, value_rows, counts, levels, gate_table)
    ])


def solution(mesh):
    placed = (P("span", "seq", None), P("span", "seq", None), P("span", "seq", None), P(), P(), P())
    return jax.shard_map(
        body, mesh=mesh, in_specs=placed, out_specs=P("span", "seq", None), check_vma=False
    )
```

```python
import functools
import math

import jax
import jax.numpy as jnp
from jax import lax
from jax.experimental import pallas as pl
from jax.experimental.pallas import tpu as pltpu
from jax.sharding import PartitionSpec as P

HEAD_DIM = 128
EPSILON = 1e-5
MASKED = -1e30
LOWEST = -1e4
TINY = 1e-30
MESH = pl.DeviceIdType.MESH
VMEM_BYTES = 32 * 1024 * 1024


def kernel(
    spans, z_far, side, tok,
    query_ref, key_ref, value_ref, counts_ref, levels_ref, gate_ref, out_ref,
    key_rows, query_rows, paired, paired_in, key_all, query_all, value_all, keys_flat, values_flat, chances, summed, part, part_in, lse, lse_in,
    mixed, gate_v, counts_s, levels_s,
    load_sems, send_sem, recv_sem, key_sems, query_sems, value_sems, part_sems, lse_sems,
    out_send, out_recv, small_sems,
):
    column = spans * z_far
    half_size = column // 2
    near = z_far // 2
    rows = z_far * tok
    many = side * rows
    pairs = spans // 2
    span = lax.axis_index("span")
    seq = lax.axis_index("seq")
    z_hi = lax.rem(seq, z_far)
    plane = lax.div(seq, z_far)
    row_y, col_x = lax.div(plane, side), lax.rem(plane, side)
    core = lax.rem(span, 2)
    place = z_hi * spans + span
    key_at = jnp.where(core == 0, row_y, col_x)
    query_at = jnp.where(core == 0, col_x, row_y)
    key_step = jnp.where(core == 0, side, 1)
    query_step = jnp.where(core == 0, 1, side)
    my_half = lax.div(place, half_size)

    def at_place(other):
        return {"span": lax.rem(other, spans), "seq": plane * z_far + lax.div(other, spans)}

    def other_place(step):
        half = lax.div(step + 1, 2)
        away = column // 2 + jnp.where(lax.rem(step, 2) == 0, half, -half)
        return lax.rem(place + away, column)

    def key_peer(turn):
        other = lax.rem(key_at + turn, side)
        return {"span": span, "seq": seq + (other - key_at) * key_step * z_far}

    def query_peer(turn):
        other = lax.rem(query_at + turn, side)
        return {"span": span, "seq": seq + (other - query_at) * query_step * z_far}

    def channels(head):
        return pl.ds(pl.multiple_of(head * HEAD_DIM, HEAD_DIM), HEAD_DIM)

    barrier = pltpu.get_barrier_semaphore()

    def greet(step, carry):
        pl.semaphore_signal(barrier, inc=1, device_id=at_place(other_place(step)), device_id_type=MESH)
        return carry

    lax.fori_loop(0, column - 1, greet, 0)
    for turn in range(1, side):
        pl.semaphore_signal(barrier, inc=1, device_id=key_peer(turn), device_id_type=MESH)
        pl.semaphore_signal(barrier, inc=1, device_id=query_peer(turn), device_id_type=MESH)

    loads = []
    for n, (source, target) in enumerate(((key_ref, key_rows), (query_ref, query_rows))):
        copy = pltpu.make_async_copy(source, target, load_sems.at[n])
        copy.start()
        loads.append(copy)
    pltpu.make_async_copy(
        value_ref.at[0, :, channels(place)], value_all.at[key_at, z_hi, span], recv_sem.at[1, my_half]
    ).start()
    small = [
        pltpu.make_async_copy(counts_ref, counts_s, small_sems.at[0]),
        pltpu.make_async_copy(levels_ref, levels_s, small_sems.at[1]),
        pltpu.make_async_copy(gate_ref.at[:, channels(place)], gate_v, small_sems.at[2]),
    ]
    for copy in small:
        copy.start()
    for n, source in enumerate((key_rows, query_rows)):
        loads[n].wait()
        for head in range(column):
            paired[head, n] = source[0, :, head * HEAD_DIM : (head + 1) * HEAD_DIM]
    pltpu.make_async_copy(
        paired.at[place], paired_in.at[z_hi, span], recv_sem.at[0, my_half]
    ).start()
    pl.semaphore_wait(barrier, column - 1 + 2 * (side - 1))

    def spread_pairs(step, carry):
        other = other_place(step)
        pltpu.make_async_remote_copy(
            src_ref=paired.at[other], dst_ref=paired_in.at[z_hi, span],
            send_sem=send_sem.at[0], recv_sem=recv_sem.at[0, my_half],
            device_id=at_place(other), device_id_type=MESH,
        ).start()
        return carry

    def spread_values(step, carry):
        other = other_place(step)
        there = jnp.where(lax.rem(other, 2) == 0, row_y, col_x)
        pltpu.make_async_remote_copy(
            src_ref=value_ref.at[0, :, channels(other)], dst_ref=value_all.at[there, z_hi, span],
            send_sem=send_sem.at[1], recv_sem=recv_sem.at[1, my_half],
            device_id=at_place(other), device_id_type=MESH,
        ).start()
        return carry

    lax.fori_loop(0, column - 1, spread_pairs, 0)
    lax.fori_loop(0, column - 1, spread_values, 0)

    def gather(n, half):
        target, sems = ((key_all, key_sems), (query_all, query_sems), (value_all, value_sems))[n]
        here, peer = (query_at, query_peer) if n == 1 else (key_at, key_peer)
        slab = pl.ds(half * near, near)
        block = target.at[here, slab]
        source = block if n == 2 else paired_in.at[slab, :, n]
        copies = []
        for turn in range(1, side):
            copy = pltpu.make_async_remote_copy(
                src_ref=source, dst_ref=block, send_sem=sems.at[0, half, turn],
                recv_sem=sems.at[1, half, turn], device_id=peer(turn), device_id_type=MESH,
            )
            copy.start()
            copies.append(copy)
        if n < 2:
            target[here, half * near : (half + 1) * near] = paired_in[
                half * near : (half + 1) * near, :, n
            ]
        return copies

    def arrive(target, n, half):
        block = target.at[pl.ds(half * near, near)]
        pltpu.make_async_copy(block, block, recv_sem.at[n, half]).wait()

    first, second = [], []
    for half, copies in ((1, first), (0, second)):
        arrive(paired_in, 0, half)
        copies.append(gather(0, half))
        copies.append(gather(1, half))
    for half, copies in ((1, first), (0, second)):
        arrive(value_all.at[key_at], 1, half)
        copies.append(gather(2, half))
    for copy in small:
        copy.wait()

    block = side * near * tok
    lanes = lax.broadcasted_iota(jnp.int32, (1, 2 * block), 1)
    inside = lax.rem(lanes, block)
    start = plane + (lax.div(inside, near * tok) - key_at) * key_step
    bias = []
    for half in range(2):
        position = start * rows + half * near * tok + lax.rem(inside, near * tok)
        bias.append([
            jnp.where(
                position < jnp.where(lanes < block, counts_s[2 * j], counts_s[2 * j + 1]),
                0.0, MASKED,
            )
            for j in range(pairs)
        ])
    row_ids = lax.broadcasted_iota(jnp.int32, (many, many), 0)
    lane_ids = lax.broadcasted_iota(jnp.int32, (many, many), 1)
    diagonal = row_ids == lane_ids
    row_ids = lax.broadcasted_iota(jnp.int32, (many, 2 * block), 0)
    lane_ids = lax.broadcasted_iota(jnp.int32, (many, 2 * block), 1)
    later = jnp.where((lax.rem(lax.div(row_ids, tok), 2) == 0) & (lane_ids >= block), MASKED, 0.0)
    factor = math.log2(math.e) / math.sqrt(HEAD_DIM)

    def flat(tiles):
        wide = tiles.astype(jnp.float32)
        return wide.reshape(math.prod(wide.shape[:-1]), HEAD_DIM).astype(jnp.bfloat16)

    def flatten(source, target, half):
        for c in range(spans):
            target[half, c * block : (c + 1) * block] = flat(
                source[:, half * near : (half + 1) * near, c]
            )

    def landed(copies):
        for copy in copies:
            copy.wait_recv()

    landed(first[0])
    flatten(key_all, keys_flat, 1)
    landed(first[2])
    flatten(value_all, values_flat, 1)
    landed(first[1])
    landed(second[0])
    flatten(key_all, keys_flat, 0)
    landed(second[1])

    def exchange(source, target, sems, at):
        copies = []
        for turn in range(1, side):
            copy = pltpu.make_async_remote_copy(
                src_ref=source(lax.rem(query_at + turn, side)), dst_ref=target(turn - 1),
                send_sem=sems.at[0, at, turn], recv_sem=sems.at[1, at, turn],
                device_id=query_peer(turn), device_id_type=MESH,
            )
            copy.start()
            copies.append(copy)
        return copies

    def score(half):
        totals = []
        for j in range(pairs):
            wide = 2 * (j + 1) * block
            queries = flat(query_all[:, half * near : (half + 1) * near, 2 * j : 2 * j + 2])
            scores = []
            for part_of in range(2):
                raw = lax.dot_general(
                    queries, keys_flat[part_of, :wide], (((1,), (1,)), ((), ())),
                    preferred_element_type=jnp.float32,
                ) * factor
                for i in range(j + 1):
                    piece = raw[:, 2 * i * block : 2 * (i + 1) * block] + bias[part_of][i]
                    scores.append(piece + later if i == j else piece)
            top = functools.reduce(jnp.maximum, scores)
            top = jnp.maximum(jnp.max(top, axis=1, keepdims=True), LOWEST)
            weights = [jnp.exp2(piece - top) for piece in scores]
            total = jnp.sum(functools.reduce(jnp.add, weights), axis=1, keepdims=True)
            total = jnp.maximum(total, TINY)
            for at, piece in enumerate(weights):
                i = at % (j + 1)
                chances[half, j, at // (j + 1), :, 2 * i * block : 2 * (i + 1) * block] = (
                    piece.astype(jnp.bfloat16)
                )
            both = jnp.sum(jnp.where(diagonal, top + jnp.log2(total), 0.0), axis=0, keepdims=True)
            lse[half, j : j + 1, :] = both
            totals.append(1.0 / total)
        return totals, exchange(
            lambda other: lse.at[half], lambda n: lse_in.at[half, n], lse_sems, half
        )

    def weigh(half, j, part_of):
        wide = 2 * (j + 1) * block
        return jnp.dot(
            chances[half, j, part_of, :, :wide], values_flat[part_of, :wide],
            preferred_element_type=jnp.float32,
        )

    scored = [score(0), score(1)]
    for half in range(2):
        for j in range(pairs):
            summed[half, j] = weigh(half, j, 1)
    landed(second[2])
    flatten(value_all, values_flat, 0)

    def mix(half):
        for j in range(pairs):
            mixture = (summed[half, j] + weigh(half, j, 0)) * scored[half][0][j]
            part[half, :, :, 2 * j : 2 * j + 2] = mixture.reshape(
                side, near, 2, tok, HEAD_DIM
            ).astype(jnp.bfloat16)
        return [
            exchange(
                lambda other: part.at[half, other, z], lambda n: part_in.at[half, n, z],
                part_sems, half * near + z,
            )
            for z in range(near)
        ]

    cut = 2 * tok
    row_ids = lax.broadcasted_iota(jnp.int32, (cut, many), 0)
    lane_ids = lax.broadcasted_iota(jnp.int32, (cut, many), 1) - query_at * near * cut

    def share_out(half):
        landed(scored[half][1])
        tables = [lse[half]] + [lse_in[half, n] for n in range(side - 1)]
        top = functools.reduce(jnp.maximum, tables)
        tables = [jnp.exp2(table - top) for table in tables]
        total = functools.reduce(jnp.add, tables)
        tables = [table / total for table in tables]
        return [
            [
                jnp.concatenate([
                    jnp.sum(
                        jnp.where(lane_ids == row_ids + z * cut, table[j : j + 1], 0.0),
                        axis=1, keepdims=True,
                    )
                    for j in range(pairs)
                ], axis=0)
                for table in tables
            ]
            for z in range(near)
        ]

    parts = mix(0)
    shares = share_out(0)
    gates = jnp.concatenate([
        jnp.broadcast_to(gate_v[pl.ds(levels_s[i], 1), :], (tok, HEAD_DIM)) for i in range(spans)
    ], axis=0)
    parts += mix(1)
    shares += share_out(1)

    for level in range(z_far):
        half, z = level // near, level % near
        landed(parts[level])
        attended = jnp.zeros((spans * tok, HEAD_DIM), jnp.float32)
        for n in range(side):
            tile = part[half, query_at, z] if n == 0 else part_in[half, n - 1, z]
            tile = tile.astype(jnp.float32).reshape(spans * tok, HEAD_DIM)
            attended = attended + shares[level][n] * tile
        mean = jnp.mean(attended * attended, axis=1, keepdims=True)
        normed = attended * lax.rsqrt(mean + EPSILON) * gates
        mixed[level] = normed.reshape(spans, tok, HEAD_DIM).astype(jnp.bfloat16)

        def send_back(step, carry, level=level):
            other_span = step + 1 - 2 * lax.rem(step, 2)
            other = level * spans + other_span

            @pl.when(other != place)
            def _():
                pltpu.make_async_remote_copy(
                    src_ref=mixed.at[level, other_span],
                    dst_ref=out_ref.at[0, :, channels(place)],
                    send_sem=out_send, recv_sem=out_recv,
                    device_id=at_place(other), device_id_type=MESH,
                ).start()

            @pl.when(other == place)
            def _():
                pltpu.make_async_copy(
                    mixed.at[level, other_span], out_ref.at[0, :, channels(place)], out_recv
                ).start()

            return carry

        lax.fori_loop(0, spans, send_back, 0)

    sent = [copy for group in first + second + parts for copy in group]
    sent += scored[0][1] + scored[1][1]
    rest = paired.at[pl.ds(0, column - 1)]
    pltpu.make_async_copy(rest, rest, send_sem.at[0]).wait()
    rest = value_ref.at[0, :, pl.ds(0, (column - 1) * HEAD_DIM)]
    pltpu.make_async_copy(rest, rest, send_sem.at[1]).wait()
    for copy in sent:
        copy.wait_send()
    rest = out_ref.at[0, :, pl.ds(0, (column - 1) * HEAD_DIM)]
    pltpu.make_async_copy(rest, rest, out_send).wait()
    pltpu.make_async_copy(out_ref, out_ref, out_recv).wait()


def body(query_rows, key_rows, value_rows, counts, levels, gate_table):
    spans = lax.axis_size("span")
    seq_size = lax.axis_size("seq")
    tok, width = query_rows.shape[1:]
    column = width // HEAD_DIM
    z_far = column // spans
    side = math.isqrt(seq_size // z_far)
    many = side * z_far * tok
    pairs = spans // 2
    bf16, f32 = jnp.bfloat16, jnp.float32
    gathered = pltpu.VMEM((side, z_far, spans, tok, HEAD_DIM), bf16)
    flat = pltpu.VMEM((2, spans * many // 2, HEAD_DIM), bf16)
    dma = pltpu.SemaphoreType.DMA
    hbm = pl.BlockSpec(memory_space=pltpu.HBM)
    return pl.pallas_call(
        functools.partial(kernel, spans, z_far, side, tok),
        out_shape=jax.ShapeDtypeStruct(query_rows.shape, bf16),
        in_specs=[hbm] * 6,
        out_specs=pl.BlockSpec(memory_space=pl.ANY),
        scratch_shapes=[
            pltpu.VMEM(key_rows.shape, bf16),
            pltpu.VMEM(query_rows.shape, bf16),
            pltpu.VMEM((column, 2, tok, HEAD_DIM), bf16),
            pltpu.VMEM((z_far, spans, 2, tok, HEAD_DIM), bf16),
            gathered, gathered, gathered, flat, flat,
            pltpu.VMEM((2, pairs, 2, many, spans * many // 2), bf16),
            pltpu.VMEM((2, pairs, many, HEAD_DIM), f32),
            pltpu.VMEM((2, side, z_far // 2, spans, tok, HEAD_DIM), bf16),
            pltpu.VMEM((2, side - 1, z_far // 2, spans, tok, HEAD_DIM), bf16),
            pltpu.VMEM((2, pairs, many), f32),
            pltpu.VMEM((2, side - 1, pairs, many), f32),
            pltpu.VMEM((z_far, spans, tok, HEAD_DIM), bf16),
            pltpu.VMEM((gate_table.shape[0], HEAD_DIM), f32),
            pltpu.SMEM(counts.shape, jnp.int32),
            pltpu.SMEM(levels.shape, jnp.int32),
            dma((2,)), dma((2,)), dma((2, 2)),
            dma((2, 2, side)), dma((2, 2, side)), dma((2, 2, side)),
            dma((2, z_far, side)), dma((2, 2, side)),
            dma, dma, dma((3,)),
        ],
        compiler_params=pltpu.CompilerParams(
            collective_id=0, has_side_effects=True, vmem_limit_bytes=VMEM_BYTES
        ),
        cost_estimate=pl.CostEstimate(
            flops=600_000_000, bytes_accessed=1_000_000, transcendentals=700_000
        ),
    )(*[
        pltpu.with_memory_space_constraint(array, pltpu.HBM)
        for array in (query_rows, key_rows, value_rows, counts, levels, gate_table)
    ])


def solution(mesh):
    placed = (P("span", "seq", None), P("span", "seq", None), P("span", "seq", None), P(), P(), P())
    return jax.shard_map(
        body, mesh=mesh, in_specs=placed, out_specs=P("span", "seq", None), check_vma=False
    )
```
